32 devices in a mesh: groups: 2 (over y), heads: 4 (over z), seq: 4 (over x, core).
Axes of the slice: x: 2, y: 2, z: 4, core: 2. Of those that a mesh axis runs over, the one named last changes fastest.
Arguments:
- mixer_in: bfloat16 [4, 4096, 4096], P('groups', 'seq', 'heads'), parts along dimension 0, may hold values from -6 to 6
- cotangent: bfloat16 [4, 4096, 4096], P('groups', 'seq', 'heads'), parts along dimension 0, may hold values from -0.375 to 0.375
- b_proj: bfloat16 [4, 4096, 64], P('groups', 'seq'), parts along dimension 0, may hold values from -3 to 3
- c_proj: bfloat16 [4, 4096, 64], P('groups', 'seq'), parts along dimension 0, may hold values from -0.75 to 0.75
- log_decay: float32 [4, 64, 4096], P('groups', 'heads', 'seq'), parts along dimension 0, may hold values from -1.5 to 0
- skip_gain: float32 [64], P('heads'), may hold values from 0.25 to 1.75
- offsets: int32 [4], P('groups'), parts along dimension 0, may hold values from 0 to 3, as said below
- resets: int32 [4, 2], P('groups'), parts along dimension 0, may hold values from 1 to 4095
Outputs:
- mixed_out: bfloat16 [4, 4096, 4096], P('groups', 'seq', 'heads'), parts along dimension 0
- grad_in: bfloat16 [4, 4096, 4096], P('groups', 'seq', 'heads'), parts along dimension 0
- grad_b: float32 [4, 4096, 64], P('groups', 'seq'), parts along dimension 0
- grad_c: float32 [4, 4096, 64], P('groups', 'seq'), parts along dimension 0
The draws below stay inside these ranges and needn't reach their ends.
There are 2 independent parts, one for each index of `groups`. The reference program is written for one: setup_inputs(seed, part) draws one part's arguments, and reference() takes and returns one part's arrays. A program takes and returns all parts, laid end to end along the dimension named above; an argument that names none is the same for every part. Nothing has to cross between parts.
Inputs may be any that keep to these rules, and one draw needn't show every extreme that they name: `offsets`: the sequences start on distinct devices; one starts on device 0 and one on device 4 - 1.
All inputs are finite; a program needn't handle non-finite values.
Results may differ from the reference program's by a relative error of at most 0.0056.
Values sent between devices are 32-bit elements; how exact they have to be, the bound alone decides.
A program may use at most 192 MiB of HBM per device.

```python
import math
import jax
import jax.numpy as jnp
from jax import lax

HEADS = 64
HEAD = 64
STATE = 64
CH = 1024
SEQUENCE_COUNT = 2
RESETS = 2
SEQUENCE_LENGTH = 4096
N_SEQ = 4


def draw_offsets(key, part):
    key_middle = jax.random.fold_in(key, 101)
    key_order = jax.random.fold_in(key, 202)
    middle = 1 + jax.random.permutation(key_middle, N_SEQ - 2)[:SEQUENCE_COUNT - 2]
    values = jnp.concatenate([jnp.array([0, N_SEQ - 1], jnp.int32), middle.astype(jnp.int32)])
    order = jax.random.permutation(key_order, SEQUENCE_COUNT)
    return values[order]


def draw_log_decay(key, part):
    key_class = jax.random.fold_in(key, 11)
    key_slow = jax.random.fold_in(key, 12)
    key_fast = jax.random.fold_in(key, 13)
    key_token = jax.random.fold_in(key, 14)
    random_key_locations = jax.random.fold_in(key, 15)
    key_depth = jax.random.fold_in(key, 16)
    full_shape = (SEQUENCE_COUNT, HEADS, SEQUENCE_LENGTH)
    fast = jax.random.bernoulli(key_class, 0.5, (SEQUENCE_COUNT, HEADS, 1))
    token_symbol = jnp.exp(jax.random.uniform(key_token, full_shape, jnp.float32, math.log(0.5), math.log(2.0)))
    slow_rate = jnp.exp(jax.random.uniform(key_slow, (SEQUENCE_COUNT, HEADS, 1), jnp.float32, math.log(0.1 / SEQUENCE_LENGTH), math.log(0.8 / SEQUENCE_LENGTH)))
    fast_rate = jnp.exp(jax.random.uniform(key_fast, (SEQUENCE_COUNT, HEADS, 1), jnp.float32, math.log(1.0 / 50.0), math.log(1.0 / 30.0)))
    baseline_probability = jnp.where(fast, fast_rate, slow_rate)
    cluster_location = jax.random.randint(random_key_locations, (SEQUENCE_COUNT, 2, 1), 0, SEQUENCE_LENGTH)
    token_offset = jnp.arange(SEQUENCE_LENGTH, dtype=jnp.int32)
    cluster_triggered = token_offset[None, None, :] == cluster_location
    nesting_level = jax.random.uniform(key_depth, (SEQUENCE_COUNT, 2, 1), jnp.float32, 0.22, 0.69)
    reset_cluster = jnp.sum(jnp.where(cluster_triggered, nesting_level, 0.0), axis=1)
    return (-(baseline_probability * token_symbol) - reset_cluster[:, None, :]).astype(jnp.float32)


def with_ends(drawn, own_key, least, top_value):
    longest = drawn.shape.index(max(drawn.shape))
    spots = []
    for shift in (0, 1):
        where = [jax.random.randint(jax.random.fold_in(own_key, axis), (), 0, length) for axis, length in enumerate(drawn.shape)]
        where[longest] = (where[longest] + shift) % drawn.shape[longest]
        spots.append(tuple(where))
    return drawn.at[spots[0]].set(least).at[spots[1]].set(top_value)


def block_levels(own_key, dims, cuts, low, largest):
    def one(dim, shards_of):
        steps = jax.random.uniform(jax.random.fold_in(jax.random.fold_in(own_key, 6), dim), (shards_of,), jnp.float32, low / len(cuts), largest / len(cuts))
        return jnp.repeat(jnp.exp(steps), dims[dim] // shards_of).reshape((-1,) + (1,) * (len(dims) - dim - 1))

    factor_of = one(*cuts[0])
    for cut in cuts[1:]:
        factor_of = factor_of * one(*cut)
    return factor_of


def scatter_about(key, dims, width, reach, shards=(), kind=jnp.bfloat16):
    drawn = width * jax.random.normal(key, dims, jnp.float32)
    if shards:
        drawn = drawn * block_levels(key, dims, shards, -0.22, 0.18)
    return jnp.clip(drawn, -reach, reach).astype(kind)


def setup_inputs(seed: int = 0, part: int = 0) -> dict:
    seeds = jax.random.split(jax.random.key(seed), 9)
    own_keys = jax.random.split(jax.random.fold_in(seeds[8], part), 9)
    return {
        "mixer_in": scatter_about(own_keys[0], (SEQUENCE_COUNT, SEQUENCE_LENGTH, HEADS * HEAD), 1.0, 6.0, ((1, 4), (2, 4))),
        "cotangent": scatter_about(own_keys[1], (SEQUENCE_COUNT, SEQUENCE_LENGTH, HEADS * HEAD), 0.0625, 0.375, ((1, 4), (2, 4))),
        "b_proj": scatter_about(own_keys[2], (SEQUENCE_COUNT, SEQUENCE_LENGTH, STATE), 0.5, 3.0, ((1, 4),)),
        "c_proj": scatter_about(own_keys[3], (SEQUENCE_COUNT, SEQUENCE_LENGTH, STATE), STATE ** -0.5, 0.75, ((1, 4),)),
        "log_decay": draw_log_decay(jax.random.fold_in(jax.random.fold_in(seeds[8], part), 71), part),
        "skip_gain": jnp.clip(1.0 + 0.15 * jax.random.normal(seeds[5], (HEADS,), jnp.float32), 0.25, 1.75),
        "offsets": draw_offsets(jax.random.fold_in(jax.random.fold_in(seeds[8], part), 71), part),
        "resets": with_ends(jax.random.randint(own_keys[7], (SEQUENCE_COUNT, RESETS), 1, SEQUENCE_LENGTH), jax.random.fold_in(own_keys[7], 1), 1, SEQUENCE_LENGTH - 1).astype(jnp.int32),
    }


def block_local(inputs_head, cot_head, b_rows, c_rows, decay_row, skip_value, doc_ids, gram, prev_doc, next_doc):
    block_len = decay_row.shape[0]
    cum_log = jnp.cumsum(decay_row)
    excl_log = cum_log - decay_row
    total_log = cum_log[block_len - 1]
    input_scale = jnp.sqrt(-jnp.expm1(2.0 * decay_row))
    same_doc = doc_ids[:, None] == doc_ids[None, :]
    row_index = lax.broadcasted_iota(jnp.int32, (block_len, block_len), 0)
    col_index = lax.broadcasted_iota(jnp.int32, (block_len, block_len), 1)
    causal = jnp.where(same_doc & (col_index <= row_index), jnp.exp(jnp.minimum(cum_log[:, None] - cum_log[None, :], 0.0)), 0.0)
    anticausal = jnp.where(same_doc & (col_index >= row_index), jnp.exp(jnp.minimum(excl_log[None, :] - excl_log[:, None], 0.0)), 0.0)
    mixing = causal + anticausal
    scaled = (input_scale[:, None] * inputs_head).astype(jnp.bfloat16)
    mixed_gram = (mixing * gram).astype(jnp.bfloat16)
    inner_prod = jnp.dot(cot_head, scaled.T, preferred_element_type=jnp.float32)
    mixed_inner = (mixing * inner_prod).astype(jnp.bfloat16)
    out_local = jnp.dot(mixed_gram, scaled, preferred_element_type=jnp.float32) + skip_value * inputs_head
    grad_local = input_scale[:, None] * jnp.dot(mixed_gram.T, cot_head, preferred_element_type=jnp.float32) + skip_value * cot_head
    gradb_local = jnp.dot(mixed_inner.T, c_rows, preferred_element_type=jnp.float32)
    gradc_local = jnp.dot(mixed_inner, b_rows, preferred_element_type=jnp.float32)
    last_doc = doc_ids[block_len - 1]
    first_doc = doc_ids[0]
    keep_last = (doc_ids == last_doc).astype(jnp.float32)
    keep_first = (doc_ids == first_doc).astype(jnp.float32)
    weight_h = (b_rows * (jnp.exp(total_log - cum_log) * keep_last)[:, None]).astype(jnp.bfloat16)
    weight_m = (c_rows * (jnp.exp(total_log - excl_log) * keep_last)[:, None]).astype(jnp.bfloat16)
    weight_g = (b_rows * (jnp.exp(excl_log) * keep_first)[:, None]).astype(jnp.bfloat16)
    weight_l = (c_rows * (jnp.exp(cum_log) * keep_first)[:, None]).astype(jnp.bfloat16)
    state_h = jnp.dot(weight_h.T, scaled, preferred_element_type=jnp.float32)
    state_m = jnp.dot(weight_m.T, cot_head, preferred_element_type=jnp.float32)
    state_g = jnp.dot(weight_g.T, scaled, preferred_element_type=jnp.float32)
    state_l = jnp.dot(weight_l.T, cot_head, preferred_element_type=jnp.float32)
    fwd_local = jnp.concatenate([state_h, state_m], axis=1)
    bwd_local = jnp.concatenate([state_g, state_l], axis=1)
    fwd_factor = jnp.exp(total_log) * (last_doc == prev_doc).astype(jnp.float32)
    bwd_factor = jnp.exp(total_log) * (first_doc == next_doc).astype(jnp.float32)
    prev_keep = (doc_ids == prev_doc).astype(jnp.float32)
    next_keep = (doc_ids == next_doc).astype(jnp.float32)
    coefs = jnp.stack([jnp.exp(cum_log) * prev_keep, jnp.exp(excl_log) * prev_keep, jnp.exp(total_log - excl_log) * next_keep, jnp.exp(total_log - cum_log) * next_keep])
    return (out_local, grad_local, gradb_local, gradc_local, fwd_local, bwd_local, fwd_factor, bwd_factor, coefs, input_scale, scaled)

def finish(out_local, grad_local, gradb_local, gradc_local, coefs, input_scale, scaled, cot_head, b_rows, c_rows, fwd_in, bwd_in):
    head_dim = cot_head.shape[1]
    state_h = fwd_in[:, :head_dim].astype(jnp.bfloat16)
    state_m = fwd_in[:, head_dim:].astype(jnp.bfloat16)
    state_g = bwd_in[:, :head_dim].astype(jnp.bfloat16)
    state_l = bwd_in[:, head_dim:].astype(jnp.bfloat16)
    alpha = coefs[0][:, None]
    delta = coefs[1][:, None]
    beta = coefs[2][:, None]
    gamma = coefs[3][:, None]
    mixed = out_local + alpha * jnp.dot(c_rows, state_h, preferred_element_type=jnp.float32) + beta * jnp.dot(c_rows, state_g, preferred_element_type=jnp.float32)
    grad = grad_local + input_scale[:, None] * (gamma * jnp.dot(b_rows, state_l, preferred_element_type=jnp.float32) + delta * jnp.dot(b_rows, state_m, preferred_element_type=jnp.float32))
    grad_bb = gradb_local + gamma * jnp.dot(scaled, state_l.T, preferred_element_type=jnp.float32) + delta * jnp.dot(scaled, state_m.T, preferred_element_type=jnp.float32)
    grad_cc = gradc_local + alpha * jnp.dot(cot_head, state_h.T, preferred_element_type=jnp.float32) + beta * jnp.dot(cot_head, state_g.T, preferred_element_type=jnp.float32)
    return (mixed.astype(jnp.bfloat16), grad.astype(jnp.bfloat16), grad_bb, grad_cc)

def head_pass(inputs_head, cot_head, decay_rows, skip_value, b_seq, c_seq, doc_ids, gram, prev_doc, next_doc):
    pieces = jax.vmap(block_local, in_axes=(0, 0, 0, 0, 0, None, 0, 0, 0, 0))(inputs_head, cot_head, b_seq, c_seq, decay_rows, skip_value, doc_ids, gram, prev_doc, next_doc)
    fwd_local = pieces[4]
    bwd_local = pieces[5]

    def forward(carried, element):
        return (element[1] * carried + element[0], carried)
    zero_state = jnp.zeros(fwd_local.shape[1:], jnp.float32)
    _, fwd_in = lax.scan(forward, zero_state, (fwd_local, pieces[6]))
    _, bwd_in = lax.scan(forward, zero_state, (bwd_local, pieces[7]), reverse=True)
    return jax.vmap(finish)(pieces[0], pieces[1], pieces[2], pieces[3], pieces[8], pieces[9], pieces[10], cot_head, b_seq, c_seq, fwd_in, bwd_in)

def reference(mixer_in, cotangent, b_proj, c_proj, log_decay, skip_gain, offsets, resets):
    block_ids = jnp.arange(N_SEQ, dtype=jnp.int32)
    token_offset = jnp.arange(N_SEQ * CH, dtype=jnp.int32)
    mixed_list = []
    grad_list = []
    gradb_list = []
    gradc_list = []
    for seq_id in range(SEQUENCE_COUNT):
        shift_by = offsets[seq_id] * CH
        inputs_seq = jnp.roll(mixer_in[seq_id], -shift_by, axis=0).reshape(N_SEQ, CH, HEADS, HEAD).transpose(2, 0, 1, 3)
        cot_seq = jnp.roll(cotangent[seq_id], -shift_by, axis=0).reshape(N_SEQ, CH, HEADS, HEAD).transpose(2, 0, 1, 3)
        b_seq = jnp.roll(b_proj[seq_id], -shift_by, axis=0).reshape(N_SEQ, CH, STATE)
        c_seq = jnp.roll(c_proj[seq_id], -shift_by, axis=0).reshape(N_SEQ, CH, STATE)
        decay_seq = jnp.roll(log_decay[seq_id], -shift_by, axis=1).reshape(HEADS, N_SEQ, CH)
        bounds = resets[seq_id]
        doc_ids = lax.optimization_barrier(jnp.sum((token_offset[:, None] >= bounds[None, :]).astype(jnp.int32), axis=1)).reshape(N_SEQ, CH)
        starts = block_ids * CH
        prev_doc = lax.optimization_barrier(jnp.sum(((starts - 1)[:, None] >= bounds[None, :]).astype(jnp.int32), axis=1))
        next_doc = lax.optimization_barrier(jnp.sum(((starts + CH)[:, None] >= bounds[None, :]).astype(jnp.int32), axis=1))
        gram = jnp.einsum('ktn,kun->ktu', c_seq.astype(jnp.float32), b_seq.astype(jnp.float32), precision=lax.Precision.HIGHEST)

        def per_head(element):
            return head_pass(element[0], element[1], element[2], element[3], b_seq, c_seq, doc_ids, gram, prev_doc, next_doc)
        mixed_h, grad_h, gradb_h, gradc_h = lax.map(per_head, (inputs_seq, cot_seq, decay_seq, skip_gain))
        mixed_list.append(jnp.roll(mixed_h.transpose(1, 2, 0, 3).reshape(N_SEQ * CH, HEADS * HEAD), shift_by, axis=0))
        grad_list.append(jnp.roll(grad_h.transpose(1, 2, 0, 3).reshape(N_SEQ * CH, HEADS * HEAD), shift_by, axis=0))
        gradb_list.append(jnp.roll(lax.optimization_barrier(jnp.sum(gradb_h, axis=0)).reshape(N_SEQ * CH, STATE), shift_by, axis=0))
        gradc_list.append(jnp.roll(lax.optimization_barrier(jnp.sum(gradc_h, axis=0)).reshape(N_SEQ * CH, STATE), shift_by, axis=0))
    return (jnp.stack(mixed_list), jnp.stack(grad_list), jnp.stack(gradb_list), jnp.stack(gradc_list))
```

```python
import jax
import jax.numpy as jnp
from jax import lax
from jax.experimental import pallas as pl
from jax.experimental.pallas import tpu as pltpu
from jax.sharding import PartitionSpec as P

Q = 128
LOG2E = 1.4426950408889634
QUANTITIES = 11
A2, E2, SCALE, WH, WM, WG, WL, ALPHA, DELTA, BETA, GAMMA = range(QUANTITIES)
DOC = 2 * QUANTITIES
ROWS = 24
F32 = jnp.float32
BF16 = jnp.bfloat16


def dot(x, y):
    return jnp.dot(x, y, preferred_element_type=F32)


def dot_nt(x, y):
    return lax.dot_general(x, y, (((1,), (1,)), ((), ())), preferred_element_type=F32)


def dot_tn(x, y):
    return lax.dot_general(x, y, (((0,), (0,)), ((), ())), preferred_element_type=F32)


def lane_first(head_dim):
    return lax.broadcasted_iota(jnp.int32, (Q, 2 * head_dim), 1) < head_dim


def spread(cols, quantity, first):
    at = 2 * quantity
    return jnp.where(first, cols[:, at : at + 1], cols[:, at + 1 : at + 2])


def split_heads(pair, first):
    zero = jnp.zeros_like(pair)
    return jnp.concatenate([jnp.where(first, pair, zero), jnp.where(first, zero, pair)], axis=0)


def positions():
    row = lax.broadcasted_iota(jnp.int32, (Q, Q), 0)
    col = lax.broadcasted_iota(jnp.int32, (Q, Q), 1)
    return row, col


def doc_mask(rows, cols, row, col):
    same = cols[:, DOC : DOC + 1] == rows[DOC : DOC + 1, :]
    return jnp.where(same, jnp.where(row == col, 2.0, 1.0), 0.0)


def states_kernel(x_ref, cot_ref, b_ref, c_ref, rows_ref, fac_ref, fwd_ref, bwd_ref, loc_ref):
    chunks = rows_ref.shape[2]
    pair = x_ref.shape[2]
    first = lane_first(pair // 2)
    bx = []
    cc = []
    for k in range(chunks):
        at = pl.ds(k * Q, Q)
        cols = rows_ref[0, 0, k].T
        scaled = (spread(cols, SCALE, first) * x_ref[0, at, :].astype(F32)).astype(BF16).astype(F32)
        cot = cot_ref[0, at, :].astype(F32)
        weighted = jnp.concatenate(
            [
                (spread(cols, WH, first) * scaled).astype(BF16),
                (spread(cols, WG, first) * scaled).astype(BF16),
            ],
            axis=1,
        )
        bx.append(dot_tn(b_ref[0, at, :], weighted))
        weighted = jnp.concatenate(
            [
                (spread(cols, WM, first) * cot).astype(BF16),
                (spread(cols, WL, first) * cot).astype(BF16),
            ],
            axis=1,
        )
        cc.append(dot_tn(c_ref[0, at, :], weighted))
    h = jnp.zeros((bx[0].shape[0], pair), F32)
    m = h
    for k in range(chunks):
        loc_ref[0, 0, k, :, 0:pair] = h.astype(BF16)
        loc_ref[0, 0, k, :, 2 * pair : 3 * pair] = m.astype(BF16)
        f = fac_ref[0, 0, 0, k : k + 1, :]
        h = f * h + bx[k][:, :pair]
        m = f * m + cc[k][:, :pair]
    fwd_ref[0, 0, :, 0:pair] = h
    fwd_ref[0, 0, :, pair : 2 * pair] = m
    g = jnp.zeros_like(h)
    l = g
    for k in reversed(range(chunks)):
        loc_ref[0, 0, k, :, pair : 2 * pair] = g.astype(BF16)
        loc_ref[0, 0, k, :, 3 * pair : 4 * pair] = l.astype(BF16)
        f = fac_ref[0, 0, 1, k : k + 1, :]
        g = f * g + bx[k][:, pair:]
        l = f * l + cc[k][:, pair:]
    bwd_ref[0, 0, :, 0:pair] = g
    bwd_ref[0, 0, :, pair : 2 * pair] = l


def local_grads_kernel(x_ref, cot_ref, b_ref, c_ref, rows_ref, out_ref, total):
    chunks = rows_ref.shape[2]
    first = lane_first(x_ref.shape[2] // 2)
    row, col = positions()
    lower = row >= col
    step = pl.program_id(1)

    @pl.when(step == 0)
    def _():
        total[...] = jnp.zeros_like(total)

    for k in range(chunks):
        at = pl.ds(k * Q, Q)
        rows = rows_ref[0, 0, k]
        cols = rows.T
        scaled = (spread(cols, SCALE, first) * x_ref[0, at, :].astype(F32)).astype(BF16)
        inner = dot_nt(cot_ref[0, at, :], split_heads(scaled, first))
        added = total[k]
        for h in range(2):
            a = 2 * A2 + h
            e = 2 * E2 + h
            decay = jnp.exp2(
                jnp.where(
                    lower,
                    cols[:, a : a + 1] - rows[a : a + 1, :],
                    rows[e : e + 1, :] - cols[:, e : e + 1],
                )
            )
            added = added + decay * inner[:, h * Q : (h + 1) * Q]
        total[k] = added

    @pl.when(step == pl.num_programs(1) - 1)
    def _():
        for k in range(chunks):
            at = pl.ds(k * Q, Q)
            rows = rows_ref[0, 0, k]
            mixed = (total[k] * doc_mask(rows, rows.T, row, col)).astype(BF16)
            grad_b = dot_tn(mixed, c_ref[0, at, :])
            grad_c = dot(mixed, b_ref[0, at, :])
            out_ref[0, at, :] = jnp.concatenate([grad_b, grad_c], axis=1)


def chunk_states(loc_ref, fac_ref, fwd_ref, bwd_ref):
    chunks = loc_ref.shape[2]
    pair = fac_ref.shape[4]
    ahead = []
    factor = jnp.ones((1, pair), F32)
    for k in range(chunks):
        ahead.append(factor)
        factor = factor * fac_ref[0, 0, 0, k : k + 1, :]
    behind = [None] * chunks
    factor = jnp.ones((1, pair), F32)
    for k in reversed(range(chunks)):
        behind[k] = factor
        factor = factor * fac_ref[0, 0, 1, k : k + 1, :]
    states = []
    for k in range(chunks):
        parts = []
        for i, (ref, factors) in enumerate(((fwd_ref, ahead), (bwd_ref, behind)) * 2):
            kept = loc_ref[0, 0, k, :, i * pair : (i + 1) * pair].astype(F32)
            half = (i // 2) * pair
            parts.append((kept + factors[k] * ref[0, 0, :, half : half + pair]).astype(BF16))
        states.append(
            (jnp.concatenate(parts[:2], axis=1), jnp.concatenate(parts[2:], axis=1))
        )
    return states


def far_grads_kernel(x_ref, cot_ref, rows_ref, fac_ref, loc_ref, fwd_ref, bwd_ref, near_ref, out_ref):
    chunks = rows_ref.shape[2]
    first = lane_first(x_ref.shape[2] // 2)
    states = chunk_states(loc_ref, fac_ref, fwd_ref, bwd_ref)

    @pl.when(pl.program_id(1) == 0)
    def _():
        out_ref[...] = near_ref[...]

    for k in range(chunks):
        at = pl.ds(k * Q, Q)
        cols = rows_ref[0, 0, k].T
        scaled = (spread(cols, SCALE, first) * x_ref[0, at, :].astype(F32)).astype(BF16).astype(F32)
        cot = cot_ref[0, at, :].astype(F32)
        state_hg, state_ml = states[k]
        weighted = jnp.concatenate(
            [
                (spread(cols, ALPHA, first) * cot).astype(BF16),
                (spread(cols, BETA, first) * cot).astype(BF16),
            ],
            axis=1,
        )
        grad_c = dot_nt(weighted, state_hg)
        weighted = jnp.concatenate(
            [
                (spread(cols, DELTA, first) * scaled).astype(BF16),
                (spread(cols, GAMMA, first) * scaled).astype(BF16),
            ],
            axis=1,
        )
        grad_b = dot_nt(weighted, state_ml)
        out_ref[0, at, :] += jnp.concatenate([grad_b, grad_c], axis=1)


def rows_out_kernel(
    x_ref, cot_ref, b_ref, c_ref, rows_ref, fac_ref, loc_ref, fwd_ref, bwd_ref, skip_ref,
    mixed_ref, grad_ref, gram, gram_t,
):
    chunks = rows_ref.shape[2]
    pair = x_ref.shape[2]
    first = lane_first(pair // 2)
    row, col = positions()
    states = chunk_states(loc_ref, fac_ref, fwd_ref, bwd_ref)
    skip = skip_ref[0]

    @pl.when(pl.program_id(1) == 0)
    def _():
        for k in range(chunks):
            at = pl.ds(k * Q, Q)
            rows = rows_ref[0, 0, k]
            mask = doc_mask(rows, rows.T, row, col)
            gram[k] = dot_nt(c_ref[0, at, :], b_ref[0, at, :]) * mask
            gram_t[k] = dot_nt(b_ref[0, at, :], c_ref[0, at, :]) * mask

    for k in range(chunks):
        at = pl.ds(k * Q, Q)
        rows = rows_ref[0, 0, k]
        cols = rows.T
        x = x_ref[0, at, :].astype(F32)
        scale = spread(cols, SCALE, first)
        scaled = (scale * x).astype(BF16)
        cot = cot_ref[0, at, :]
        near = []
        near_t = []
        for h in range(2):
            a = 2 * A2 + h
            e = 2 * E2 + h
            a_diff = cols[:, a : a + 1] - rows[a : a + 1, :]
            e_diff = rows[e : e + 1, :] - cols[:, e : e + 1]
            decay = jnp.exp2(jnp.where(row >= col, a_diff, e_diff))
            decay_t = jnp.exp2(-jnp.where(row <= col, a_diff, e_diff))
            near.append((decay * gram[k]).astype(BF16))
            near_t.append((decay_t * gram_t[k]).astype(BF16))
        mixed = dot(jnp.concatenate(near, axis=1), split_heads(scaled, first))
        grad = dot(jnp.concatenate(near_t, axis=1), split_heads(cot, first))
        state_hg, state_ml = states[k]
        far = dot(c_ref[0, at, :], state_hg)
        mixed = mixed + spread(cols, ALPHA, first) * far[:, :pair]
        mixed = mixed + spread(cols, BETA, first) * far[:, pair:]
        mixed_ref[0, at, :] = (mixed + skip * x).astype(BF16)
        far = dot(b_ref[0, at, :], state_ml)
        grad = grad + spread(cols, DELTA, first) * far[:, :pair]
        grad = grad + spread(cols, GAMMA, first) * far[:, pair:]
        grad_ref[0, at, :] = (scale * grad + skip * cot.astype(F32)).astype(BF16)


def exchange(fwd, bwd, factors, core, chip, chips):
    axis = "seq"
    count = 2 * chips
    half = fwd.shape[2] // 2
    swap = [(i, i ^ 1) for i in range(count)]
    own = jnp.stack([fwd, bwd])
    is_even = core == 0
    low, high = own[:, :, :, :half], own[:, :, :, half:]
    mine = jnp.where(is_even, low, high)
    given = jnp.where(is_even, high, low)
    other = lax.ppermute(given, axis, swap)
    even = jnp.where(is_even, mine, other)
    odd = jnp.where(is_even, other, mine)
    factors = factors.reshape((chips, 2) + factors.shape[1:])

    def at(place, direction):
        return lax.dynamic_index_in_dim(factors, jnp.mod(place, chips), 0, keepdims=False)[:, direction]

    here_f = at(chip, 0)
    here_b = at(chip, 1)
    chip_f = odd[0] + here_f[1] * even[0]
    chip_b = even[1] + here_b[0] * odd[1]
    now_f, now_b = chip_f, chip_b
    sum_f = sum_b = None
    weight_f = weight_b = None
    for step in range(1, chips + 1):
        if step < chips:
            now_f = lax.ppermute(now_f, axis, [(i, (i + 2) % count) for i in range(count)])
            now_b = lax.ppermute(now_b, axis, [(i, (i - 2) % count) for i in range(count)])
        else:
            now_f, now_b = chip_f, chip_b
        if step == 1:
            sum_f, sum_b = now_f, now_b
        else:
            sum_f = sum_f + weight_f * now_f
            sum_b = sum_b + weight_b * now_b
        next_f = at(chip - step, 0)
        next_b = at(chip + step, 1)
        next_f = next_f[0] * next_f[1]
        next_b = next_b[0] * next_b[1]
        weight_f = next_f if weight_f is None else weight_f * next_f
        weight_b = next_b if weight_b is None else weight_b * next_b
    into_even = jnp.stack([sum_f, odd[1] + here_b[1] * sum_b])
    into_odd = jnp.stack([even[0] + here_f[0] * sum_f, sum_b])
    kept = jnp.where(is_even, into_even, into_odd)
    got = lax.ppermute(jnp.where(is_even, into_odd, into_even), axis, swap)
    low = jnp.where(is_even, kept, got)
    high = jnp.where(is_even, got, kept)
    return jnp.concatenate([low, high], axis=3)


def per_device(mixer_in, cotangent, b_proj, c_proj, log_decay, skip_gain, offsets, resets):
    seqs, length, width = mixer_in.shape
    heads = log_decay.shape[1]
    head_dim = width // heads
    state = b_proj.shape[2]
    pair = 2 * head_dim
    pairs = heads // 2
    chunks = length // Q
    devices = lax.axis_size("seq")
    place = lax.axis_index("seq")

    block = jnp.mod(place - offsets, devices)
    start = block * length
    bounds = resets[:, None, :]

    def doc_at(position):
        return jnp.sum((position[:, :, None] >= bounds).astype(jnp.int32), axis=2)

    doc = doc_at(start[:, None] + jnp.arange(length, dtype=jnp.int32)[None, :]).reshape(seqs, chunks, Q)
    chunk_start = start[:, None] + Q * jnp.arange(chunks, dtype=jnp.int32)[None, :]
    prev_doc = doc_at(chunk_start - 1)
    next_doc = doc_at(chunk_start + Q)
    first_doc = doc_at(chunk_start)
    last_doc = doc_at(chunk_start + Q - 1)

    decay = log_decay.reshape(seqs, pairs, 2, chunks, Q).transpose(0, 1, 3, 2, 4)
    triangle = (jnp.arange(Q)[:, None] <= jnp.arange(Q)[None, :]).astype(F32)
    cum = jnp.einsum("spkhu,ut->spkht", decay, triangle, precision=lax.Precision.HIGHEST)
    excl = cum - decay
    total = cum[..., Q - 1 :]

    def keep(which):
        return (doc == which[:, :, None]).astype(F32)[:, None, :, None, :]

    keep_last, keep_first, keep_prev, keep_next = map(keep, (last_doc, first_doc, prev_doc, next_doc))
    from_cum, from_excl = jnp.exp(total - cum), jnp.exp(total - excl)
    to_cum, to_excl = jnp.exp(cum), jnp.exp(excl)
    rows = jnp.concatenate(
        [
            cum * LOG2E,
            excl * LOG2E,
            jnp.sqrt(-jnp.expm1(2.0 * decay)),
            from_cum * keep_last,
            from_excl * keep_last,
            to_excl * keep_first,
            to_cum * keep_first,
            to_cum * keep_prev,
            to_excl * keep_prev,
            from_excl * keep_next,
            from_cum * keep_next,
            jnp.broadcast_to(
                doc.astype(F32)[:, None, :, None, :], (seqs, pairs, chunks, ROWS - DOC, Q)
            ),
        ],
        axis=3,
    )
    whole = jnp.exp(total[..., 0])
    passing = jnp.stack([last_doc == prev_doc, first_doc == next_doc], axis=1).astype(F32)
    by_head = whole[:, :, None] * passing[:, None, :, :, None]
    factors = jnp.repeat(by_head, head_dim, axis=-1)

    alive = jnp.stack([block != 0, block != devices - 1]).astype(F32)
    chain = jnp.prod(by_head, axis=3).transpose(2, 0, 1, 3) * alive[:, :, None, None]
    chain = lax.all_gather(chain, "seq")
    chain = jnp.tile(jnp.repeat(chain, head_dim, axis=-1), 2)[..., None, :]

    wide = pl.BlockSpec((1, length, pair), lambda s, p: (s, 0, p))
    thin = pl.BlockSpec((1, length, state), lambda s, p: (s, 0, 0))
    row_spec = pl.BlockSpec((1, 1, chunks, ROWS, Q), lambda s, p: (s, p, 0, 0, 0))
    fac_spec = pl.BlockSpec((1, 1, 2, chunks, pair), lambda s, p: (s, p, 0, 0, 0))
    state_spec = pl.BlockSpec((1, 1, state, 2 * pair), lambda s, p: (s, p, 0, 0))
    loc_spec = pl.BlockSpec((1, 1, chunks, state, 4 * pair), lambda s, p: (s, p, 0, 0, 0))
    sum_spec = pl.BlockSpec((1, length, 2 * state), lambda s, p: (s, 0, 0))
    skip_spec = pl.BlockSpec((1, 1, pair), lambda s, p: (p, 0, 0))
    grid = (seqs, pairs)
    params = pltpu.CompilerParams(vmem_limit_bytes=40 * 2**20)

    def cost(flops, moved):
        return pl.CostEstimate(flops=int(flops), bytes_accessed=int(moved), transcendentals=0)

    area = seqs * length * width
    state_shape = jax.ShapeDtypeStruct((seqs, pairs, state, 2 * pair), F32)
    fwd, bwd, local = pl.pallas_call(
        states_kernel,
        grid=grid,
        in_specs=[wide, wide, thin, thin, row_spec, fac_spec],
        out_specs=[state_spec, state_spec, loc_spec],
        out_shape=[
            state_shape,
            state_shape,
            jax.ShapeDtypeStruct((seqs, pairs, chunks, state, 4 * pair), BF16),
        ],
        compiler_params=params,
        cost_estimate=cost(8 * area * state, 8 * area),
        name="states",
    )(mixer_in, cotangent, b_proj, c_proj, rows, factors)

    near = pl.pallas_call(
        local_grads_kernel,
        grid=grid,
        in_specs=[wide, wide, thin, thin, row_spec],
        out_specs=sum_spec,
        out_shape=jax.ShapeDtypeStruct((seqs, length, 2 * state), F32),
        scratch_shapes=[pltpu.VMEM((chunks, Q, Q), F32)],
        compiler_params=params,
        cost_estimate=cost(6000 * area, 4 * area),
        name="near_grads",
    )(mixer_in, cotangent, b_proj, c_proj, rows)

    incoming = exchange(fwd, bwd, chain, jnp.mod(place, 2), place // 2, devices // 2)
    incoming = incoming * alive[:, :, None, None, None]

    grads = pl.pallas_call(
        far_grads_kernel,
        grid=grid,
        in_specs=[wide, wide, row_spec, fac_spec, loc_spec, state_spec, state_spec, sum_spec],
        out_specs=sum_spec,
        out_shape=jax.ShapeDtypeStruct((seqs, length, 2 * state), F32),
        compiler_params=params,
        cost_estimate=cost(8 * area * state, 8 * area),
        name="far_grads",
    )(mixer_in, cotangent, rows, factors, local, incoming[0], incoming[1], near)
    grads = lax.psum(grads, "heads")

    skip = jnp.repeat(skip_gain.reshape(pairs, 1, 2), head_dim, axis=-1)
    mixed, grad_in = pl.pallas_call(
        rows_out_kernel,
        grid=grid,
        in_specs=[
            wide, wide, thin, thin, row_spec, fac_spec, loc_spec, state_spec, state_spec, skip_spec,
        ],
        out_specs=[wide, wide],
        out_shape=[jax.ShapeDtypeStruct(mixer_in.shape, BF16)] * 2,
        scratch_shapes=[pltpu.VMEM((chunks, Q, Q), F32)] * 2,
        compiler_params=params,
        cost_estimate=cost(12000 * area, 10 * area),
        name="rows_out",
    )(mixer_in, cotangent, b_proj, c_proj, rows, factors, local, incoming[0], incoming[1], skip)
    return mixed, grad_in, grads[..., :state], grads[..., state:]


def solution(mesh):
    placed = (
        P("groups", "seq", "heads"),
        P("groups", "seq", "heads"),
        P("groups", "seq", None),
        P("groups", "seq", None),
        P("groups", "heads", "seq"),
        P("heads"),
        P("groups"),
        P("groups", None),
    )
    return jax.shard_map(
        per_device,
        mesh=mesh,
        in_specs=placed,
        out_specs=(
            P("groups", "seq", "heads"),
            P("groups", "seq", "heads"),
            P("groups", "seq", None),
            P("groups", "seq", None),
        ),
        check_vma=False,
    )
```

```python
import numpy as np

import jax
import jax.numpy as jnp
from jax import lax
from jax.experimental import pallas as pl
from jax.experimental.pallas import tpu as pltpu
from jax.sharding import PartitionSpec as P

Q = 128
LOG2E = 1.4426950408889634
QUANTITIES = 11
A2, E2, SCALE, WH, WM, WG, WL, ALPHA, DELTA, BETA, GAMMA = range(QUANTITIES)
DOC = 2 * QUANTITIES
ROWS = 24
F32 = jnp.float32
BF16 = jnp.bfloat16


def dot(x, y):
    return jnp.dot(x, y, preferred_element_type=F32)


def dot_nt(x, y):
    return lax.dot_general(x, y, (((1,), (1,)), ((), ())), preferred_element_type=F32)


def dot_tn(x, y):
    return lax.dot_general(x, y, (((0,), (0,)), ((), ())), preferred_element_type=F32)


def lane_first(head_dim):
    return lax.broadcasted_iota(jnp.int32, (Q, 2 * head_dim), 1) < head_dim


def selector(wanted, head_dim):
    out = np.zeros((ROWS, len(wanted), 2 * head_dim), np.float32)
    for i, (quantity, head) in enumerate(wanted):
        if head is None:
            out[2 * quantity, i, :head_dim] = 1.0
            out[2 * quantity + 1, i, head_dim:] = 1.0
        else:
            out[2 * quantity + head, i, :] = 1.0
    out = out.reshape(ROWS, -1)
    return jnp.asarray(np.concatenate([out] * 3, axis=0), BF16)


def columns(rows, select_ref):
    high = rows.astype(BF16).astype(F32)
    rest = rows - high
    middle = rest.astype(BF16).astype(F32)
    parts = jnp.concatenate([high, middle, rest - middle], axis=0).astype(BF16)
    spread = dot_tn(parts, select_ref[...])
    return [spread[:, i : i + Q] for i in range(0, spread.shape[1], Q)]


def split_heads(pair, first):
    zero = jnp.zeros_like(pair)
    return jnp.concatenate([jnp.where(first, pair, zero), jnp.where(first, zero, pair)], axis=0)


def positions():
    row = lax.broadcasted_iota(jnp.int32, (Q, Q), 0)
    col = lax.broadcasted_iota(jnp.int32, (Q, Q), 1)
    return row, col


def doc_mask(rows, cols, row, col):
    same = cols[:, DOC : DOC + 1] == rows[DOC : DOC + 1, :]
    return jnp.where(same, jnp.where(row == col, 2.0, 1.0), 0.0)


def states_kernel(x_ref, cot_ref, b_ref, c_ref, rows_ref, fac_ref, select_ref, fwd_ref, bwd_ref, loc_ref):
    chunks = rows_ref.shape[2]
    pair = x_ref.shape[2]
    bx = []
    cc = []
    for k in range(chunks):
        at = pl.ds(k * Q, Q)
        scale, w_h, w_g, w_m, w_l = columns(rows_ref[0, 0, k], select_ref)
        scaled = (scale * x_ref[0, at, :].astype(F32)).astype(BF16).astype(F32)
        cot = cot_ref[0, at, :].astype(F32)
        weighted = jnp.concatenate(
            [
                (w_h * scaled).astype(BF16),
                (w_g * scaled).astype(BF16),
            ],
            axis=1,
        )
        bx.append(dot_tn(b_ref[0, at, :], weighted))
        weighted = jnp.concatenate(
            [
                (w_m * cot).astype(BF16),
                (w_l * cot).astype(BF16),
            ],
            axis=1,
        )
        cc.append(dot_tn(c_ref[0, at, :], weighted))
    h = jnp.zeros((bx[0].shape[0], pair), F32)
    m = h
    for k in range(chunks):
        loc_ref[0, 0, k, :, 0:pair] = h.astype(BF16)
        loc_ref[0, 0, k, :, 2 * pair : 3 * pair] = m.astype(BF16)
        f = fac_ref[0, 0, 0, k : k + 1, :]
        h = f * h + bx[k][:, :pair]
        m = f * m + cc[k][:, :pair]
    fwd_ref[0, 0, :, 0:pair] = h
    fwd_ref[0, 0, :, pair : 2 * pair] = m
    g = jnp.zeros_like(h)
    l = g
    for k in reversed(range(chunks)):
        loc_ref[0, 0, k, :, pair : 2 * pair] = g.astype(BF16)
        loc_ref[0, 0, k, :, 3 * pair : 4 * pair] = l.astype(BF16)
        f = fac_ref[0, 0, 1, k : k + 1, :]
        g = f * g + bx[k][:, pair:]
        l = f * l + cc[k][:, pair:]
    bwd_ref[0, 0, :, 0:pair] = g
    bwd_ref[0, 0, :, pair : 2 * pair] = l


def local_grads_kernel(x_ref, cot_ref, b_ref, c_ref, rows_ref, select_ref, out_ref, total):
    chunks = rows_ref.shape[2]
    first = lane_first(x_ref.shape[2] // 2)
    row, col = positions()
    lower = row >= col
    step = pl.program_id(1)

    @pl.when(step == 0)
    def _():
        total[...] = jnp.zeros_like(total)

    for k in range(chunks):
        at = pl.ds(k * Q, Q)
        rows = rows_ref[0, 0, k]
        scale, *sides = columns(rows, select_ref)
        scaled = (scale * x_ref[0, at, :].astype(F32)).astype(BF16)
        inner = dot_nt(cot_ref[0, at, :], split_heads(scaled, first))
        added = total[k]
        for h in range(2):
            a = 2 * A2 + h
            e = 2 * E2 + h
            decay = jnp.exp2(
                jnp.where(
                    lower,
                    sides[h] - rows[a : a + 1, :],
                    rows[e : e + 1, :] - sides[2 + h],
                )
            )
            added = added + decay * inner[:, h * Q : (h + 1) * Q]
        total[k] = added

    @pl.when(step == pl.num_programs(1) - 1)
    def _():
        for k in range(chunks):
            at = pl.ds(k * Q, Q)
            rows = rows_ref[0, 0, k]
            mixed = (total[k] * doc_mask(rows, rows.T, row, col)).astype(BF16)
            grad_b = dot_tn(mixed, c_ref[0, at, :])
            grad_c = dot(mixed, b_ref[0, at, :])
            out_ref[0, at, :] = jnp.concatenate([grad_b, grad_c], axis=1)


def chunk_states(loc_ref, fac_ref, fwd_ref, bwd_ref):
    chunks = loc_ref.shape[2]
    pair = fac_ref.shape[4]
    ahead = []
    factor = jnp.ones((1, pair), F32)
    for k in range(chunks):
        ahead.append(factor)
        factor = factor * fac_ref[0, 0, 0, k : k + 1, :]
    behind = [None] * chunks
    factor = jnp.ones((1, pair), F32)
    for k in reversed(range(chunks)):
        behind[k] = factor
        factor = factor * fac_ref[0, 0, 1, k : k + 1, :]
    states = []
    for k in range(chunks):
        parts = []
        for i, (ref, factors) in enumerate(((fwd_ref, ahead), (bwd_ref, behind)) * 2):
            kept = loc_ref[0, 0, k, :, i * pair : (i + 1) * pair].astype(F32)
            half = (i // 2) * pair
            parts.append((kept + factors[k] * ref[0, 0, :, half : half + pair]).astype(BF16))
        states.append(
            (jnp.concatenate(parts[:2], axis=1), jnp.concatenate(parts[2:], axis=1))
        )
    return states


def far_grads_kernel(
    x_ref, cot_ref, rows_ref, fac_ref, loc_ref, fwd_ref, bwd_ref, near_ref, select_ref, out_ref
):
    chunks = rows_ref.shape[2]
    states = chunk_states(loc_ref, fac_ref, fwd_ref, bwd_ref)

    @pl.when(pl.program_id(1) == 0)
    def _():
        out_ref[...] = near_ref[...]

    for k in range(chunks):
        at = pl.ds(k * Q, Q)
        scale, alpha, beta, delta, gamma = columns(rows_ref[0, 0, k], select_ref)
        scaled = (scale * x_ref[0, at, :].astype(F32)).astype(BF16).astype(F32)
        cot = cot_ref[0, at, :].astype(F32)
        state_hg, state_ml = states[k]
        weighted = jnp.concatenate(
            [
                (alpha * cot).astype(BF16),
                (beta * cot).astype(BF16),
            ],
            axis=1,
        )
        grad_c = dot_nt(weighted, state_hg)
        weighted = jnp.concatenate(
            [
                (delta * scaled).astype(BF16),
                (gamma * scaled).astype(BF16),
            ],
            axis=1,
        )
        grad_b = dot_nt(weighted, state_ml)
        out_ref[0, at, :] += jnp.concatenate([grad_b, grad_c], axis=1)


def rows_out_kernel(
    x_ref, cot_ref, b_ref, c_ref, rows_ref, fac_ref, loc_ref, fwd_ref, bwd_ref, skip_ref, select_ref,
    mixed_ref, grad_ref, gram, gram_t,
):
    chunks = rows_ref.shape[2]
    pair = x_ref.shape[2]
    first = lane_first(pair // 2)
    row, col = positions()
    states = chunk_states(loc_ref, fac_ref, fwd_ref, bwd_ref)
    skip = skip_ref[0]

    @pl.when(pl.program_id(1) == 0)
    def _():
        for k in range(chunks):
            at = pl.ds(k * Q, Q)
            rows = rows_ref[0, 0, k]
            mask = doc_mask(rows, rows.T, row, col)
            gram[k] = dot_nt(c_ref[0, at, :], b_ref[0, at, :]) * mask
            gram_t[k] = dot_nt(b_ref[0, at, :], c_ref[0, at, :]) * mask

    for k in range(chunks):
        at = pl.ds(k * Q, Q)
        rows = rows_ref[0, 0, k]
        scale, alpha, beta, delta, gamma, *sides = columns(rows, select_ref)
        x = x_ref[0, at, :].astype(F32)
        scaled = (scale * x).astype(BF16)
        cot = cot_ref[0, at, :]
        near = []
        near_t = []
        for h in range(2):
            a = 2 * A2 + h
            e = 2 * E2 + h
            a_diff = sides[h] - rows[a : a + 1, :]
            e_diff = rows[e : e + 1, :] - sides[2 + h]
            decay = jnp.exp2(jnp.where(row >= col, a_diff, e_diff))
            decay_t = jnp.exp2(-jnp.where(row <= col, a_diff, e_diff))
            near.append((decay * gram[k]).astype(BF16))
            near_t.append((decay_t * gram_t[k]).astype(BF16))
        mixed = dot(jnp.concatenate(near, axis=1), split_heads(scaled, first))
        grad = dot(jnp.concatenate(near_t, axis=1), split_heads(cot, first))
        state_hg, state_ml = states[k]
        far = dot(c_ref[0, at, :], state_hg)
        mixed = mixed + alpha * far[:, :pair]
        mixed = mixed + beta * far[:, pair:]
        mixed_ref[0, at, :] = (mixed + skip * x).astype(BF16)
        far = dot(b_ref[0, at, :], state_ml)
        grad = grad + delta * far[:, :pair]
        grad = grad + gamma * far[:, pair:]
        grad_ref[0, at, :] = (scale * grad + skip * cot.astype(F32)).astype(BF16)


def exchange(fwd, bwd, factors, core, chips, meanwhile):
    axis = "seq"
    count = 2 * chips
    half = fwd.shape[2] // 2
    swap = [(i, i ^ 1) for i in range(count)]
    own = jnp.stack([fwd, bwd])
    is_even = core == 0
    low, high = own[:, :, :, :half], own[:, :, :, half:]
    mine = jnp.where(is_even, low, high)
    given = jnp.where(is_even, high, low)
    other = lax.ppermute(given, axis, swap)
    even = jnp.where(is_even, mine, other)
    odd = jnp.where(is_even, other, mine)
    def at(hops, direction):
        return [
            jnp.where(is_even, factors[(2 * hops - k) % count], factors[(2 * hops + 1 - k) % count])[direction]
            for k in range(2)
        ]

    here_f = at(0, 0)
    here_b = at(0, 1)
    chip_f = odd[0] + here_f[1] * even[0]
    chip_b = even[1] + here_b[0] * odd[1]
    near, (chip_f, chip_b) = meanwhile((chip_f, chip_b))
    now_f, now_b = chip_f, chip_b
    sum_f = sum_b = None
    weight_f = weight_b = None
    for step in range(1, chips + 1):
        if step < chips:
            now_f = lax.ppermute(now_f, axis, [(i, (i + 2) % count) for i in range(count)])
            now_b = lax.ppermute(now_b, axis, [(i, (i - 2) % count) for i in range(count)])
            if step == 1:
                now_f, now_b, near = lax.optimization_barrier((now_f, now_b, near))
        else:
            now_f, now_b = chip_f, chip_b
        if step == 1:
            sum_f, sum_b = now_f, now_b
        else:
            sum_f = sum_f + weight_f * now_f
            sum_b = sum_b + weight_b * now_b
        next_f = at(step, 0)
        next_b = at(-step, 1)
        next_f = next_f[0] * next_f[1]
        next_b = next_b[0] * next_b[1]
        weight_f = next_f if weight_f is None else weight_f * next_f
        weight_b = next_b if weight_b is None else weight_b * next_b
    into_even = jnp.stack([sum_f, odd[1] + here_b[1] * sum_b])
    into_odd = jnp.stack([even[0] + here_f[0] * sum_f, sum_b])
    kept = jnp.where(is_even, into_even, into_odd)
    got = lax.ppermute(jnp.where(is_even, into_odd, into_even), axis, swap)
    low = jnp.where(is_even, kept, got)
    high = jnp.where(is_even, got, kept)
    return jnp.concatenate([low, high], axis=3), near


def per_device(mixer_in, cotangent, b_proj, c_proj, log_decay, skip_gain, offsets, resets):
    seqs, length, width = mixer_in.shape
    heads = log_decay.shape[1]
    head_dim = width // heads
    state = b_proj.shape[2]
    pair = 2 * head_dim
    pairs = heads // 2
    chunks = length // Q
    devices = lax.axis_size("seq")
    place = lax.axis_index("seq")

    block = jnp.mod(place - offsets, devices)
    start = block * length
    bounds = resets[:, None, :]

    def doc_at(position):
        return jnp.sum((position[:, :, None] >= bounds).astype(jnp.int32), axis=2)

    doc = doc_at(start[:, None] + jnp.arange(length, dtype=jnp.int32)[None, :]).reshape(seqs, chunks, Q)
    chunk_start = start[:, None] + Q * jnp.arange(chunks, dtype=jnp.int32)[None, :]
    prev_doc = doc_at(chunk_start - 1)
    next_doc = doc_at(chunk_start + Q)
    first_doc = doc_at(chunk_start)
    last_doc = doc_at(chunk_start + Q - 1)

    decay = log_decay.reshape(seqs, pairs, 2, chunks, Q).transpose(0, 1, 3, 2, 4)
    triangle = (jnp.arange(Q)[:, None] <= jnp.arange(Q)[None, :]).astype(F32)
    cum = jnp.einsum("spkhu,ut->spkht", decay, triangle, precision=lax.Precision.HIGHEST)
    excl = cum - decay
    total = cum[..., Q - 1 :]

    def keep(which):
        return (doc == which[:, :, None]).astype(F32)[:, None, :, None, :]

    keep_last, keep_first, keep_prev, keep_next = map(keep, (last_doc, first_doc, prev_doc, next_doc))
    from_cum, from_excl = jnp.exp(total - cum), jnp.exp(total - excl)
    to_cum, to_excl = jnp.exp(cum), jnp.exp(excl)
    rows = jnp.concatenate(
        [
            cum * LOG2E,
            excl * LOG2E,
            jnp.sqrt(-jnp.expm1(2.0 * decay)),
            from_cum * keep_last,
            from_excl * keep_last,
            to_excl * keep_first,
            to_cum * keep_first,
            to_cum * keep_prev,
            to_excl * keep_prev,
            from_excl * keep_next,
            from_cum * keep_next,
            jnp.broadcast_to(
                doc.astype(F32)[:, None, :, None, :], (seqs, pairs, chunks, ROWS - DOC, Q)
            ),
        ],
        axis=3,
    )
    whole = jnp.exp(total[..., 0])
    passing = jnp.stack([last_doc == prev_doc, first_doc == next_doc], axis=1).astype(F32)
    by_head = whole[:, :, None] * passing[:, None, :, :, None]
    factors = jnp.repeat(by_head, head_dim, axis=-1)

    alive = jnp.stack([block != 0, block != devices - 1]).astype(F32)
    chain = jnp.prod(by_head, axis=3).transpose(2, 0, 1, 3) * alive[:, :, None, None]
    around = [chain] + [
        lax.ppermute(chain, "seq", [(i, (i + shift) % devices) for i in range(devices)])
        for shift in range(1, devices)
    ]
    chain = jnp.tile(jnp.repeat(jnp.stack(around), head_dim, axis=-1), 2)[..., None, :]

    wide = pl.BlockSpec((1, length, pair), lambda s, p: (s, 0, p))
    thin = pl.BlockSpec((1, length, state), lambda s, p: (s, 0, 0))
    row_spec = pl.BlockSpec((1, 1, chunks, ROWS, Q), lambda s, p: (s, p, 0, 0, 0))
    fac_spec = pl.BlockSpec((1, 1, 2, chunks, pair), lambda s, p: (s, p, 0, 0, 0))
    state_spec = pl.BlockSpec((1, 1, state, 2 * pair), lambda s, p: (s, p, 0, 0))
    loc_spec = pl.BlockSpec((1, 1, chunks, state, 4 * pair), lambda s, p: (s, p, 0, 0, 0))
    sum_spec = pl.BlockSpec((1, length, 2 * state), lambda s, p: (s, 0, 0))
    skip_spec = pl.BlockSpec((1, 1, pair), lambda s, p: (p, 0, 0))
    grid = (seqs, pairs)
    params = pltpu.CompilerParams(vmem_limit_bytes=60 * 2**20)

    def cost(flops, moved):
        return pl.CostEstimate(flops=int(flops), bytes_accessed=int(moved), transcendentals=0)

    def select(*wanted):
        matrix = selector(wanted, head_dim)
        return matrix, pl.BlockSpec(matrix.shape, lambda s, p: (0, 0))

    scale = [(SCALE, None)]
    far_factors = [(q, None) for q in (ALPHA, BETA, DELTA, GAMMA)]
    sides = [(A2, 0), (A2, 1), (E2, 0), (E2, 1)]
    states_sel, states_spec = select(*scale, *[(q, None) for q in (WH, WG, WM, WL)])
    near_sel, near_spec = select(*scale, *sides)
    far_sel, far_spec = select(*scale, *far_factors)
    out_sel, out_spec = select(*scale, *far_factors, *sides)

    area = seqs * length * width
    state_shape = jax.ShapeDtypeStruct((seqs, pairs, state, 2 * pair), F32)
    fwd, bwd, local = pl.pallas_call(
        states_kernel,
        grid=grid,
        in_specs=[wide, wide, thin, thin, row_spec, fac_spec, states_spec],
        out_specs=[state_spec, state_spec, loc_spec],
        out_shape=[
            state_shape,
            state_shape,
            jax.ShapeDtypeStruct((seqs, pairs, chunks, state, 4 * pair), BF16),
        ],
        compiler_params=params,
        cost_estimate=cost(5000 * area, 8 * area),
        name="states",
    )(mixer_in, cotangent, b_proj, c_proj, rows, factors, states_sel)

    near_call = pl.pallas_call(
        local_grads_kernel,
        grid=grid,
        in_specs=[wide, wide, thin, thin, row_spec, near_spec],
        out_specs=sum_spec,
        out_shape=jax.ShapeDtypeStruct((seqs, length, 2 * state), F32),
        scratch_shapes=[pltpu.VMEM((chunks, Q, Q), F32)],
        compiler_params=params,
        cost_estimate=cost(6000 * area, 4 * area),
        name="near_grads",
    )

    def near_grads(token):
        held, token = lax.optimization_barrier((rows, token))
        return near_call(mixer_in, cotangent, b_proj, c_proj, held, near_sel), token

    incoming, near = exchange(
        fwd, bwd, chain, jnp.mod(place, 2), devices // 2, near_grads
    )
    incoming = incoming * alive[:, :, None, None, None]

    grads = pl.pallas_call(
        far_grads_kernel,
        grid=grid,
        in_specs=[wide, wide, row_spec, fac_spec, loc_spec, state_spec, state_spec, sum_spec, far_spec],
        out_specs=sum_spec,
        out_shape=jax.ShapeDtypeStruct((seqs, length, 2 * state), F32),
        compiler_params=params,
        cost_estimate=cost(5000 * area, 8 * area),
        name="far_grads",
    )(mixer_in, cotangent, rows, factors, local, incoming[0], incoming[1], near, far_sel)
    grads = lax.psum(grads, "heads")

    skip = jnp.repeat(skip_gain.reshape(pairs, 1, 2), head_dim, axis=-1)
    mixed, grad_in = pl.pallas_call(
        rows_out_kernel,
        grid=grid,
        in_specs=[
            wide, wide, thin, thin, row_spec, fac_spec, loc_spec, state_spec, state_spec, skip_spec, out_spec,
        ],
        out_specs=[wide, wide],
        out_shape=[jax.ShapeDtypeStruct(mixer_in.shape, BF16)] * 2,
        scratch_shapes=[pltpu.VMEM((chunks, Q, Q), F32)] * 2,
        compiler_params=params,
        cost_estimate=cost(12000 * area, 10 * area),
        name="rows_out",
    )(mixer_in, cotangent, b_proj, c_proj, rows, factors, local, incoming[0], incoming[1], skip, out_sel)
    return mixed, grad_in, grads[..., :state], grads[..., state:]


def solution(mesh):
    placed = (
        P("groups", "seq", "heads"),
        P("groups", "seq", "heads"),
        P("groups", "seq", None),
        P("groups", "seq", None),
        P("groups", "heads", "seq"),
        P("heads"),
        P("groups"),
        P("groups", None),
    )
    return jax.shard_map(
        per_device,
        mesh=mesh,
        in_specs=placed,
        out_specs=(
            P("groups", "seq", "heads"),
            P("groups", "seq", "heads"),
            P("groups", "seq", None),
            P("groups", "seq", None),
        ),
        check_vma=False,
    )
```
